32 devices in a mesh: groups: 1, expert: 16 (over z, y, core), section: 2 (over x), dp: 1.
Axes of the slice: x: 2, y: 2, z: 4, core: 2. Of those that a mesh axis runs over, the one named last changes fastest.
Arguments:
- saved_input: bfloat16 [2, 2048, 1440], P('section', ('groups', 'expert')), may hold values from -6 to 6
- grad_output: bfloat16 [2, 2048, 1440], P('section', ('groups', 'expert')), may hold values from -6 to 6
- expert_ids: int32 [2, 2048, 4], P('section', ('groups', 'expert')), may hold values from 0 to 7, all different within a row; in each aligned block of 128 rows (0 to 127, 128 to 255, ..., all dimensions but the last counted through in order) at most 68 rows name the same one
- router_logits: float32 [2, 2048, 4], P('section', ('groups', 'expert')), may hold values from -6 to 6
- w_gate: bfloat16 [2, 16, 1440, 720], P('section', 'expert', None, 'dp'), may hold values from -0.15625 to 0.15625
- w_up: bfloat16 [2, 16, 1440, 720], P('section', 'expert', None, 'dp'), may hold values from -0.15625 to 0.15625
- w_down: bfloat16 [2, 16, 720, 1440], P('section', 'expert', 'dp'), may hold values from -0.15625 to 0.15625
Outputs:
- passed: bfloat16 [2, 2048, 1440], P('section', ('groups', 'expert'))
The draws below stay inside these ranges and needn't reach their ends.
Inputs may be any that keep to these rules, and one draw needn't show every extreme that they name: `expert_ids`: in each aligned block of 128 tokens (the tokens of one index of the expert axis) of a layer, no expert is named by more than 68 entries, a bound that some block reaches. A token names 4 different experts.
All inputs are finite; a program needn't handle non-finite values.
Results may differ from the reference program's by a relative error of at most 0.0057.
Values may be sent and summed in bfloat16 or wider, within the bound.
A program may use at most 64 MiB of HBM per device.

```python
import math
import jax
import jax.numpy as jnp
import numpy as np
from jax import lax

D = 1440
H = 1440
TOK_DEV = 128
EXPERTS = 8
TOP = 4
CAP = 68
LAYERS = 2
SLICES = 16
TOKENS = 2048
N_EXPERT = 16


def levels(stream_key, dims, pieces, low, top_value):
    def one(dim, parts):
        draws = jax.random.uniform(jax.random.fold_in(jax.random.fold_in(stream_key, 6), dim), (parts,), jnp.float32, low / len(pieces), top_value / len(pieces))
        return jnp.repeat(jnp.exp(draws), dims[dim] // parts).reshape((-1,) + (1,) * (len(dims) - dim - 1))

    gain = one(*pieces[0])
    for cut in pieces[1:]:
        gain = gain * one(*cut)
    return gain


def assign_block(own_key, own, number, rows, amount, top, limit, skew):
    ranking = jax.random.permutation(own_key, amount)
    crowded, common = shares(amount, rows * top, limit, skew, True), shares(amount, rows * top, limit, skew, False)
    places = jnp.arange(amount)

    def named(tallies, offset_by):
        used = int((tallies > 0).sum())
        fixed = max(1, used // 4)
        shifted = fixed + (places - fixed + offset_by * (used - fixed)) % max(1, amount - fixed)
        return jnp.zeros((amount,), jnp.int32).at[ranking[jnp.where(places < fixed, places, shifted)]].set(jnp.asarray(tallies, jnp.int32))

    tallies = jnp.where(number % 4 == 0, named(crowded, number // 4), named(common, number - number // 4 - 1))
    mixed = jax.random.permutation(jax.random.fold_in(own, 3), amount)
    giver, receiver = mixed[0:amount // 2 * 2:2], mixed[1:amount // 2 * 2:2]
    room = jnp.minimum(tallies[giver] - 1, limit - tallies[receiver]) // 2
    room = jnp.where((giver == ranking[0]) | (receiver == ranking[0]) | (tallies[receiver] == 0), 0, jnp.maximum(room, 0))
    shifted = jax.random.randint(jax.random.fold_in(own, 4), (amount // 2,), 0, 1 << 20) % (room + 1)
    tallies = tallies.at[giver].add(-shifted).at[receiver].add(shifted)
    items = jnp.searchsorted(jnp.cumsum(tallies), jnp.arange(rows * top), side="right").astype(jnp.int32)
    table = items.reshape(top, rows).T
    table = table[jax.random.permutation(jax.random.fold_in(own, 1), rows)]
    offset_by = jax.random.randint(jax.random.fold_in(own, 2), (rows, 1), 0, top)
    return jnp.take_along_axis(table, (jnp.arange(top)[None, :] + offset_by) % top, axis=1)


def shares(number_of, total, reach, skew, full):
    portions = [(1 << 20) // math.isqrt(grade ** skew) + 1 for grade in range(1, number_of + 1)]
    largest = reach if full else min(reach, max(-(-total // number_of), total * portions[0] // sum(portions)))
    least = 1 if total - largest >= number_of - 1 else 0
    counts, spare = [largest] + [least] * (number_of - 1), total - largest - least * (number_of - 1)
    while spare > 0:
        candidates = [i for i in range(1, number_of) if counts[i] < largest] or [i for i in range(1, number_of) if counts[i] < reach]
        whole, left = sum([portions[i] for i in candidates]), spare
        for i in candidates:
            more = min(reach - counts[i], max(1, left * portions[i] // whole), spare)
            counts[i] = counts[i] + more
            spare = spare - more
    return np.array(counts)


def bell_draw(rng, dims, spread, most, cuts=(), kind=jnp.bfloat16):
    gain = levels(rng, dims, cuts, -0.22, 0.18) if cuts else 1.0
    values = jax.random.normal(rng, dims, jnp.float32) * spread * gain
    return jnp.minimum(jnp.maximum(values, -most), most).astype(kind)


def setup_inputs(seed: int = 0, part: int = 0) -> dict:
    seeds = jax.random.split(jax.random.key(seed), 8)
    own_keys = jax.random.split(jax.random.fold_in(seeds[7], part), 8)
    saved_input = bell_draw(own_keys[0], (LAYERS, TOKENS, D), 1.0, 6.0, ((0, 2), (1, 16)))
    grad_output = bell_draw(own_keys[1], (LAYERS, TOKENS, D), 1.0, 6.0, ((0, 2), (1, 16)))
    expert_ids_keys = jax.random.split(jax.random.fold_in(own_keys[2], 1), LAYERS * TOKENS // TOK_DEV)
    expert_ids_turns = jax.random.permutation(jax.random.fold_in(own_keys[2], 3), LAYERS * TOKENS // TOK_DEV)
    expert_ids = jax.vmap(lambda own, number: assign_block(jax.random.fold_in(own_keys[2], 2), own, number, TOK_DEV, EXPERTS, TOP, CAP, 2))(expert_ids_keys, expert_ids_turns).reshape((LAYERS, TOKENS, TOP))
    router_logits = bell_draw(own_keys[3], (LAYERS, TOKENS, TOP), 1.0, 6.0, ((0, 2), (1, 16)), jnp.float32)
    w_gate = bell_draw(seeds[4], (LAYERS, SLICES, D, H // 2), D ** -0.5, 0.15625, ((0, 2), (1, 16)))
    w_up = bell_draw(seeds[5], (LAYERS, SLICES, D, H // 2), D ** -0.5, 0.15625, ((0, 2), (1, 16)))
    w_down = bell_draw(seeds[6], (LAYERS, SLICES, H // 2, D), H ** -0.5, 0.15625, ((0, 2), (1, 16)))
    return dict(saved_input=saved_input, grad_output=grad_output, expert_ids=expert_ids, router_logits=router_logits, w_gate=w_gate, w_up=w_up, w_down=w_down)


swish_alpha = 1.702


def reference(saved_input, grad_output, expert_ids, router_logits, w_gate, w_up, w_down):
    bound = N_EXPERT * CAP
    stacked = []
    for layer in range(LAYERS):
        feats = saved_input[layer]
        grads = grad_output[layer]
        entries = expert_ids[layer].reshape(-1).astype(jnp.int32)
        total_items = entries.shape[0]
        gate_all = w_gate[layer].reshape(EXPERTS, 2, D, H // 2).transpose(0, 2, 1, 3).reshape(EXPERTS, D, H)
        up_all = w_up[layer].reshape(EXPERTS, 2, D, H // 2).transpose(0, 2, 1, 3).reshape(EXPERTS, D, H)
        down_all = w_down[layer].reshape(EXPERTS, H, D)

        def one_expert(packed):
            index, gate_mat, up_mat, down_mat = packed
            member = jnp.nonzero(entries == index, size=bound, fill_value=total_items)[0].astype(jnp.int32)
            rows = jnp.minimum(member // TOP, TOKENS - 1).astype(jnp.int32)
            gate_pre = jnp.dot(feats[rows], gate_mat, preferred_element_type=jnp.float32)
            up_pre = jnp.dot(feats[rows], up_mat, preferred_element_type=jnp.float32)
            hidden_grad = jnp.dot(grads[rows], down_mat.T, preferred_element_type=jnp.float32)
            squash = jax.nn.sigmoid(swish_alpha * gate_pre)
            slope = squash + swish_alpha * gate_pre * squash * (1.0 - squash)
            gate_grad = (hidden_grad * (up_pre + 1.0) * slope).astype(jnp.bfloat16)
            up_grad = (hidden_grad * gate_pre * squash).astype(jnp.bfloat16)
            slot_grad = jnp.dot(gate_grad, gate_mat.T, preferred_element_type=jnp.float32)
            slot_grad = slot_grad + jnp.dot(up_grad, up_mat.T, preferred_element_type=jnp.float32)
            return member, slot_grad.astype(jnp.bfloat16)

        members, results = lax.map(one_expert, (jnp.arange(EXPERTS, dtype=jnp.int32), gate_all, up_all, down_all))
        per_item = jnp.zeros((total_items, D), jnp.bfloat16)
        per_item = per_item.at[members.reshape(-1)].set(results.reshape(-1, D), mode="drop")
        raised = jnp.exp(router_logits[layer])
        weights = raised / jnp.sum(raised, axis=1, keepdims=True)
        picked = per_item.reshape(TOKENS, TOP, D).astype(jnp.float32)
        combined = jnp.sum(weights[:, :, None] * picked, axis=1).astype(jnp.bfloat16)
        stacked.append(combined)
    return jnp.roll(jnp.stack(stacked, axis=0), -1, axis=0)
```

```python
import functools

import jax
import jax.numpy as jnp
from jax import lax
from jax.experimental import pallas as pl
from jax.experimental.pallas import tpu as pltpu
from jax.sharding import PartitionSpec as P

swish_alpha = 1.702


def swapped(value, axis, stride):
    mask = 2**stride
    pairs = [(source, source ^ mask) for source in range(lax.axis_size(axis))]
    return lax.ppermute(value, axis, pairs)


def shifted(block, axis, distance):
    devices = range(lax.axis_size(axis))
    route = [((i - distance) % len(devices), i) for i in devices]
    return lax.ppermute(block, axis, route)


def expert_rows(feat_rows, grad_rows, gate_mat, up_mat, down_mat):
    gate_pre = jnp.dot(feat_rows, gate_mat, preferred_element_type=jnp.float32)
    up_pre = jnp.dot(feat_rows, up_mat, preferred_element_type=jnp.float32)
    hidden_grad = lax.dot_general(
        grad_rows, down_mat, (((1,), (1,)), ((), ())), preferred_element_type=jnp.float32
    )
    squash = jax.nn.sigmoid(swish_alpha * gate_pre)
    slope = squash + swish_alpha * gate_pre * squash * (1.0 - squash)
    gate_grad = (hidden_grad * (up_pre + 1.0) * slope).astype(jnp.bfloat16)
    up_grad = (hidden_grad * gate_pre * squash).astype(jnp.bfloat16)
    first = lax.dot_general(
        gate_grad, gate_mat, (((1,), (1,)), ((), ())), preferred_element_type=jnp.float32
    )
    second = lax.dot_general(
        up_grad, up_mat, (((1,), (1,)), ((), ())), preferred_element_type=jnp.float32
    )
    return first + second


def on_device(saved_input, grad_output, expert_ids, router_logits, w_gate, w_up, w_down):
    gate_half = w_gate[0, 0]
    up_half = w_up[0, 0]
    down_half = w_down[0, 0]
    feat_rows = saved_input[0]
    grad_rows = grad_output[0]
    chosen = expert_ids[0]
    logits = router_logits[0]
    tokens, features = feat_rows.shape
    top_count = chosen.shape[1]
    slices = lax.axis_size("expert")
    experts = slices // 2
    capacity = min(tokens, tokens * top_count // experts * 17 // 16 // 2 * 2)
    half_cap = capacity // 2
    entries = chosen.reshape(-1)
    total_items = entries.shape[0]
    onehot = (entries[:, None] == jnp.arange(experts, dtype=jnp.int32)[None, :]).astype(jnp.int32)
    before = jnp.cumsum(onehot, axis=0) - onehot
    position = jnp.sum(before * onehot, axis=1)
    slot_of_item = entries * capacity + position
    item_of_slot = jnp.full((experts * capacity,), total_items, jnp.int32)
    item_of_slot = item_of_slot.at[slot_of_item].set(jnp.arange(total_items, dtype=jnp.int32))
    occupied = (item_of_slot < total_items)[:, None]
    source = jnp.where(item_of_slot < total_items, item_of_slot // top_count, 0)
    zero_value = jnp.zeros((), jnp.bfloat16)
    send_feats = jnp.where(occupied, feat_rows[source], zero_value).reshape(
        experts, capacity, features
    )
    send_grads = jnp.where(occupied, grad_rows[source], zero_value).reshape(
        experts, capacity, features
    )
    other_gate, other_up, other_down = swapped((gate_half, up_half, down_half), "expert", 0)
    gate_whole = jnp.concatenate([gate_half, other_gate], axis=1)
    up_whole = jnp.concatenate([up_half, other_up], axis=1)
    down_whole = jnp.concatenate([down_half, other_down], axis=0)
    split_feats = send_feats.reshape(slices, half_cap, features)
    split_grads = send_grads.reshape(slices, half_cap, features)
    got_feats = lax.all_to_all(split_feats, "expert", split_axis=0, concat_axis=0, tiled=True)
    got_grads = lax.all_to_all(split_grads, "expert", split_axis=0, concat_axis=0, tiled=True)
    senders, depth, _ = got_feats.shape
    result = expert_rows(
        got_feats.reshape(-1, features),
        got_grads.reshape(-1, features),
        gate_whole,
        up_whole,
        down_whole,
    )
    result = lax.psum(result, "dp").astype(jnp.bfloat16).reshape(senders, depth, features)
    arrived = lax.all_to_all(result, "expert", split_axis=0, concat_axis=0, tiled=True)
    slot_grad = arrived.reshape(experts * capacity, features)
    picked = slot_grad[slot_of_item].reshape(tokens, top_count, features).astype(jnp.float32)
    raised = jnp.exp(logits)
    weights = raised / jnp.sum(raised, axis=1, keepdims=True)
    combined = jnp.sum(weights[:, :, None] * picked, axis=1).astype(jnp.bfloat16)
    passed = shifted(combined, "section", -1)
    return passed[None]


MESH = pl.DeviceIdType.MESH
ROWS = 32


def dot(a, b, ca=1, cb=0):
    return lax.dot_general(a, b, (((ca,), (cb,)), ((), ())), preferred_element_type=jnp.float32)


def chain_kernel(
    n, sections, experts, cap,
    ids_ref, logits_ref, feat_hbm, grad_hbm, gate_hbm, up_hbm, down_hbm, out_ref,
    feat, grad, meta, rows_f, rows_g, send_f, send_g, res, res_in,
    part, part_send, up_in, dn_in, gate, up, down,
    own_sem, w_sem, w_send, w_recv,
    ag_recv, ag_up, ag_dn, y_send, y_recv, r_send, r_recv,
    p_send, up_recv, dn_recv, o_send, o_recv,
):
    top_count, tokens = ids_ref.shape
    me = lax.axis_index("expert")
    section = lax.axis_index("section")
    core = lax.rem(me, 2)
    e = me // 2
    y = lax.rem(e, 2)
    z = me // 4
    e_nb = e + 1 - 2 * y
    core_nb = {"expert": me + 1 - 2 * core}
    y_nb = {"expert": me + 2 - 4 * y}
    above, below = {"expert": me + 4}, {"expert": me - 4}
    before = {"section": lax.rem(section + sections - 1, sections)}
    after = {"section": lax.rem(section + 1, sections)}
    has_up, has_dn = z < n - 1, z > 0

    barrier = pltpu.get_barrier_semaphore()
    for peer in (core_nb, y_nb, before, after):
        pl.semaphore_signal(barrier, inc=1, device_id=peer, device_id_type=MESH)

    @pl.when(has_up)
    def _():
        pl.semaphore_signal(barrier, inc=1, device_id=above, device_id_type=MESH)

    @pl.when(has_dn)
    def _():
        pl.semaphore_signal(barrier, inc=1, device_id=below, device_id_type=MESH)

    raised = jnp.exp(logits_ref[...])
    weights = raised / jnp.sum(raised, axis=0, keepdims=True)
    ids = ids_ref[...]
    expert_row = lax.broadcasted_iota(jnp.int32, (experts, tokens), 0)
    chosen = jnp.zeros((experts, tokens), jnp.float32)
    weight = jnp.zeros((experts, tokens), jnp.float32)
    for k in range(top_count):
        hit = jnp.where(ids[k : k + 1, :] == expert_row, 1.0, 0.0)
        chosen = chosen + hit
        weight = weight + hit * weights[k : k + 1, :]
    earlier = lax.broadcasted_iota(jnp.int32, (tokens, tokens), 0) < lax.broadcasted_iota(
        jnp.int32, (tokens, tokens), 1
    )
    place = dot(chosen.astype(jnp.bfloat16), jnp.where(earlier, 1.0, 0.0).astype(jnp.bfloat16))
    place = jnp.where(chosen > 0.5, place, -1.0)
    meta[z, :experts, :] = weight
    meta[z, experts:, :] = place

    own_copies = [
        pltpu.make_async_copy(feat_hbm.at[0], feat.at[z], own_sem.at[0]),
        pltpu.make_async_copy(grad_hbm.at[0], grad.at[z], own_sem.at[1]),
    ]
    for copy in own_copies:
        copy.start()
    w_copies = [
        pltpu.make_async_copy(src.at[0, 0], dst.at[0], w_sem.at[j])
        for j, (src, dst) in enumerate(((gate_hbm, gate), (up_hbm, up), (down_hbm, down)))
    ]
    for copy in w_copies:
        copy.start()

    pl.semaphore_wait(
        barrier, 4 + jnp.where(has_up, 1, 0) + jnp.where(has_dn, 1, 0)
    )

    def remote(src, dst, s_sem, r_sem, peer):
        return pltpu.make_async_remote_copy(
            src_ref=src, dst_ref=dst, send_sem=s_sem, recv_sem=r_sem,
            device_id=peer, device_id_type=MESH,
        )

    buffers = (feat, grad, meta)

    def hop(kind, b, upward, src=None):
        buf = buffers[kind].at[b]
        sems = ag_up if upward else ag_dn
        return remote(
            buf if src is None else src, buf, sems.at[kind, b], ag_recv.at[kind, b],
            above if upward else below,
        )

    sources = (feat_hbm.at[0], grad_hbm.at[0], None)
    for kind in (2, 0, 1):
        @pl.when(has_up)
        def _():
            hop(kind, z, True, sources[kind]).start()

        @pl.when(has_dn)
        def _():
            hop(kind, z, False, sources[kind]).start()

    swaps = [
        remote(src.at[0, 0], dst.at[1], w_send.at[j], w_recv.at[j], core_nb)
        for j, (src, dst) in enumerate(((gate_hbm, gate), (up_hbm, up), (down_hbm, down)))
    ]
    for copy in swaps:
        copy.start()

    def block_of(k):
        near = jnp.minimum(z, n - 1 - z)
        half = (k + 1) // 2
        side = jnp.where(lax.rem(k, 2) == 1, z - half, z + half)
        far = jnp.where(z < n - 1 - z, z + k - near, z - k + near)
        return jnp.where(k <= 2 * near, side, far)

    def arrive(kind, b):
        @pl.when(b != z)
        def _():
            hop(kind, b, True).wait_recv()

        if kind < 2:
            @pl.when(b == z)
            def _():
                own_copies[kind].wait()

        @pl.when(jnp.logical_and(b < z, has_up))
        def _():
            hop(kind, b, True).start()

        @pl.when(jnp.logical_and(b > z, has_dn))
        def _():
            hop(kind, b, False).start()

    def y_copy(kind, b):
        src, dst = ((send_f, rows_f), (send_g, rows_g))[kind]
        return remote(
            src.at[b], dst.at[b, pl.ds(cap, cap)], y_send.at[kind, b], y_recv.at[kind, b], y_nb
        )

    def picks(b, expert):
        row = meta[b, pl.ds(experts + expert, 1), :]
        slot = lax.broadcasted_iota(jnp.int32, (cap, tokens), 0).astype(jnp.float32)
        return jnp.where(slot == row, 1.0, 0.0).astype(jnp.bfloat16)

    def stage_a(k):
        b = block_of(k)
        arrive(2, b)
        own, nb = picks(b, e), picks(b, e_nb)
        for kind, (whole, rows, sent) in enumerate(
            ((feat, rows_f, send_f), (grad, rows_g, send_g))
        ):
            arrive(kind, b)
            values = whole[b]
            sent[b] = dot(nb, values).astype(jnp.bfloat16)
            y_copy(kind, b).start()
            rows[b, :cap, :] = dot(own, values).astype(jnp.bfloat16)

    def r_copy(b):
        return remote(
            res.at[b, pl.ds(cap, cap)], res_in.at[b], r_send.at[b], r_recv.at[b], y_nb
        )

    def stage_b(k):
        b = block_of(k)

        @pl.when(k == 0)
        def _():
            for copy in w_copies:
                copy.wait()
            for copy in swaps:
                copy.wait_recv()

        y_copy(0, b).wait_recv()
        y_copy(1, b).wait_recv()

        def one_half(h, total):
            f, g = rows_f[b], rows_g[b]
            gate_pre = dot(f, gate[h])
            up_pre = dot(f, up[h])
            hidden_grad = dot(g, down[h], 1, 1)
            squash = jax.nn.sigmoid(swish_alpha * gate_pre)
            slope = squash + swish_alpha * gate_pre * squash * (1.0 - squash)
            gate_grad = (hidden_grad * (up_pre + 1.0) * slope).astype(jnp.bfloat16)
            up_grad = (hidden_grad * gate_pre * squash).astype(jnp.bfloat16)
            value = dot(gate_grad, gate[h], 1, 1) + dot(up_grad, up[h], 1, 1)
            return value if total is None else total + value

        total = one_half(1, one_half(0, None))
        res[b] = total.astype(jnp.bfloat16)
        r_copy(b).start()

    def p_copy(b, r, upward):
        rows = pl.ds(pl.multiple_of(r * ROWS, ROWS), ROWS)
        dst, sems = (up_in, up_recv) if upward else (dn_in, dn_recv)
        return remote(
            part_send.at[b, rows], dst.at[b, rows], p_send.at[b, r], sems.at[b, r],
            above if upward else below,
        )

    pieces = tokens // ROWS

    def stage_c(k):
        b = block_of(k)
        r_copy(b).wait_recv()
        rows = jnp.concatenate(
            [
                meta[b, pl.ds(e, 1), :],
                meta[b, pl.ds(e_nb, 1), :],
                jnp.zeros((6, tokens), jnp.float32),
            ],
            axis=0,
        )
        columns = rows.T
        value = columns[:, 0:1] * dot(picks(b, e), res[b, :cap, :], 0, 0)
        value = value + columns[:, 1:2] * dot(picks(b, e_nb), res_in[b], 0, 0)
        part[b] = value
        up_end = jnp.logical_and(b > z, jnp.logical_not(has_dn))
        dn_end = jnp.logical_and(b < z, jnp.logical_not(has_up))

        @pl.when(jnp.logical_or(up_end, dn_end))
        def _():
            part_send[b] = value.astype(jnp.bfloat16)

        @pl.when(up_end)
        def _():
            @pl.loop(0, pieces)
            def _(r):
                p_copy(b, r, True).start()

        @pl.when(dn_end)
        def _():
            @pl.loop(0, pieces)
            def _(r):
                p_copy(b, r, False).start()

    @pl.loop(0, n + 2)
    def _(k):
        @pl.when(k < n)
        def _():
            stage_a(k)

        @pl.when(jnp.logical_and(k >= 1, k <= n))
        def _():
            stage_b(k - 1)

        @pl.when(k >= 2)
        def _():
            stage_c(k - 2)

    def pass_on(b, upward):
        incoming = up_in if upward else dn_in

        @pl.loop(0, pieces)
        def _(r):
            rows = pl.ds(pl.multiple_of(r * ROWS, ROWS), ROWS)
            p_copy(b, r, upward).wait_recv()
            value = part[b, rows, :] + incoming[b, rows, :].astype(jnp.float32)
            part_send[b, rows, :] = value.astype(jnp.bfloat16)
            p_copy(b, r, upward).start()

    @pl.loop(0, n)
    def _(j):
        b = n - 1 - j

        @pl.when(jnp.logical_and(b > z, has_dn))
        def _():
            pass_on(b, True)

    @pl.loop(0, n)
    def _(b):
        @pl.when(jnp.logical_and(b < z, has_up))
        def _():
            pass_on(b, False)

    def o_copy(r):
        rows = pl.ds(pl.multiple_of(r * ROWS, ROWS), ROWS)
        return remote(
            part_send.at[z, rows], out_ref.at[0, rows], o_send.at[r], o_recv.at[r], before
        )

    @pl.loop(0, pieces)
    def _(r):
        rows = pl.ds(pl.multiple_of(r * ROWS, ROWS), ROWS)

        @pl.when(has_dn)
        def _():
            p_copy(z, r, True).wait_recv()
            part[z, rows, :] += up_in[z, rows, :].astype(jnp.float32)

        @pl.when(has_up)
        def _():
            p_copy(z, r, False).wait_recv()
            part[z, rows, :] += dn_in[z, rows, :].astype(jnp.float32)

        part_send[z, rows, :] = part[z, rows, :].astype(jnp.bfloat16)
        o_copy(r).start()

    for copy in swaps:
        copy.wait_send()

    @pl.loop(0, n)
    def _(b):
        @pl.when(jnp.logical_and(b <= z, has_up))
        def _():
            for kind in range(3):
                hop(kind, b, True).wait_send()

        @pl.when(jnp.logical_and(b >= z, has_dn))
        def _():
            for kind in range(3):
                hop(kind, b, False).wait_send()

        y_copy(0, b).wait_send()
        y_copy(1, b).wait_send()
        r_copy(b).wait_send()

        @pl.when(b != z)
        def _():
            @pl.loop(0, pieces)
            def _(r):
                p_copy(b, r, True).wait_send()

    @pl.loop(0, pieces)
    def _(r):
        o_copy(r).wait_send()
        o_copy(r).wait_recv()


def chained(saved_input, grad_output, expert_ids, router_logits, w_gate, w_up, w_down):
    _, tokens, features = saved_input.shape
    half = w_gate.shape[3]
    top_count = expert_ids.shape[2]
    slices = lax.axis_size("expert")
    experts = slices // 2
    n = slices // 4
    sections = lax.axis_size("section")
    capacity = min(tokens, tokens * top_count // experts * 17 // 16 // 2 * 2)
    cap = -(-capacity // 16) * 16
    pieces = tokens // ROWS
    bf16 = jnp.bfloat16
    dma = pltpu.SemaphoreType.DMA
    vmem, anywhere = pl.BlockSpec(memory_space=pltpu.VMEM), pl.BlockSpec(memory_space=pl.ANY)
    macs = 5 * 2 * n * cap * features * 2 * half
    return pl.pallas_call(
        functools.partial(chain_kernel, n, sections, experts, cap),
        out_shape=jax.ShapeDtypeStruct((1, tokens, features), bf16),
        in_specs=[vmem, vmem] + [anywhere] * 5,
        out_specs=anywhere,
        scratch_shapes=[
            pltpu.VMEM((n, tokens, features), bf16),
            pltpu.VMEM((n, tokens, features), bf16),
            pltpu.VMEM((n, 2 * experts, tokens), jnp.float32),
            pltpu.VMEM((n, 2 * cap, features), bf16),
            pltpu.VMEM((n, 2 * cap, features), bf16),
            pltpu.VMEM((n, cap, features), bf16),
            pltpu.VMEM((n, cap, features), bf16),
            pltpu.VMEM((n, 2 * cap, features), bf16),
            pltpu.VMEM((n, cap, features), bf16),
            pltpu.VMEM((n, tokens, features), jnp.float32),
            pltpu.VMEM((n, tokens, features), bf16),
            pltpu.VMEM((n, tokens, features), bf16),
            pltpu.VMEM((n, tokens, features), bf16),
            pltpu.VMEM((2, features, half), bf16),
            pltpu.VMEM((2, features, half), bf16),
            pltpu.VMEM((2, half, features), bf16),
            dma((2,)), dma((3,)), dma((3,)), dma((3,)),
            dma((3, n)), dma((3, n)), dma((3, n)),
            dma((2, n)), dma((2, n)), dma((n,)), dma((n,)),
            dma((n, pieces)), dma((n, pieces)), dma((n, pieces)),
            dma((pieces,)), dma((pieces,)),
        ],
        compiler_params=pltpu.CompilerParams(
            collective_id=0, has_side_effects=True, vmem_limit_bytes=58 * 1024 * 1024
        ),
        cost_estimate=pl.CostEstimate(
            flops=2 * macs, bytes_accessed=6 * half * features + 6 * tokens * features,
            transcendentals=4 * n * cap * half,
        ),
    )(expert_ids[0].T, router_logits[0].T, saved_input, grad_output, w_gate, w_up, w_down)


def solution(mesh):
    placed = (
        P("section", ("groups", "expert"), None),
        P("section", ("groups", "expert"), None),
        P("section", ("groups", "expert"), None),
        P("section", ("groups", "expert"), None),
        P("section", "expert", None, "dp"),
        P("section", "expert", None, "dp"),
        P("section", "expert", "dp", None),
    )
    shape = dict(mesh.shape)
    chain = shape["dp"] == 1 and shape["expert"] % 4 == 0 and shape["section"] > 1
    return jax.shard_map(
        chained if chain else on_device,
        mesh=mesh,
        in_specs=placed,
        out_specs=P("section", ("groups", "expert"), None),
        check_vma=False,
    )
```

```python
import functools

import jax
import jax.numpy as jnp
from jax import lax
from jax.experimental import pallas as pl
from jax.experimental.pallas import tpu as pltpu
from jax.sharding import PartitionSpec as P

swish_alpha = 1.702


def swapped(value, axis, stride):
    mask = 2**stride
    pairs = [(source, source ^ mask) for source in range(lax.axis_size(axis))]
    return lax.ppermute(value, axis, pairs)


def shifted(block, axis, distance):
    devices = range(lax.axis_size(axis))
    route = [((i - distance) % len(devices), i) for i in devices]
    return lax.ppermute(block, axis, route)


def expert_rows(feat_rows, grad_rows, gate_mat, up_mat, down_mat):
    gate_pre = jnp.dot(feat_rows, gate_mat, preferred_element_type=jnp.float32)
    up_pre = jnp.dot(feat_rows, up_mat, preferred_element_type=jnp.float32)
    hidden_grad = lax.dot_general(
        grad_rows, down_mat, (((1,), (1,)), ((), ())), preferred_element_type=jnp.float32
    )
    squash = jax.nn.sigmoid(swish_alpha * gate_pre)
    slope = squash + swish_alpha * gate_pre * squash * (1.0 - squash)
    gate_grad = (hidden_grad * (up_pre + 1.0) * slope).astype(jnp.bfloat16)
    up_grad = (hidden_grad * gate_pre * squash).astype(jnp.bfloat16)
    first = lax.dot_general(
        gate_grad, gate_mat, (((1,), (1,)), ((), ())), preferred_element_type=jnp.float32
    )
    second = lax.dot_general(
        up_grad, up_mat, (((1,), (1,)), ((), ())), preferred_element_type=jnp.float32
    )
    return first + second


def on_device(saved_input, grad_output, expert_ids, router_logits, w_gate, w_up, w_down):
    gate_half = w_gate[0, 0]
    up_half = w_up[0, 0]
    down_half = w_down[0, 0]
    feat_rows = saved_input[0]
    grad_rows = grad_output[0]
    chosen = expert_ids[0]
    logits = router_logits[0]
    tokens, features = feat_rows.shape
    top_count = chosen.shape[1]
    slices = lax.axis_size("expert")
    experts = slices // 2
    capacity = min(tokens, tokens * top_count // experts * 17 // 16 // 2 * 2)
    half_cap = capacity // 2
    entries = chosen.reshape(-1)
    total_items = entries.shape[0]
    onehot = (entries[:, None] == jnp.arange(experts, dtype=jnp.int32)[None, :]).astype(jnp.int32)
    before = jnp.cumsum(onehot, axis=0) - onehot
    position = jnp.sum(before * onehot, axis=1)
    slot_of_item = entries * capacity + position
    item_of_slot = jnp.full((experts * capacity,), total_items, jnp.int32)
    item_of_slot = item_of_slot.at[slot_of_item].set(jnp.arange(total_items, dtype=jnp.int32))
    occupied = (item_of_slot < total_items)[:, None]
    source = jnp.where(item_of_slot < total_items, item_of_slot // top_count, 0)
    zero_value = jnp.zeros((), jnp.bfloat16)
    send_feats = jnp.where(occupied, feat_rows[source], zero_value).reshape(
        experts, capacity, features
    )
    send_grads = jnp.where(occupied, grad_rows[source], zero_value).reshape(
        experts, capacity, features
    )
    other_gate, other_up, other_down = swapped((gate_half, up_half, down_half), "expert", 0)
    gate_whole = jnp.concatenate([gate_half, other_gate], axis=1)
    up_whole = jnp.concatenate([up_half, other_up], axis=1)
    down_whole = jnp.concatenate([down_half, other_down], axis=0)
    split_feats = send_feats.reshape(slices, half_cap, features)
    split_grads = send_grads.reshape(slices, half_cap, features)
    got_feats = lax.all_to_all(split_feats, "expert", split_axis=0, concat_axis=0, tiled=True)
    got_grads = lax.all_to_all(split_grads, "expert", split_axis=0, concat_axis=0, tiled=True)
    senders, depth, _ = got_feats.shape
    result = expert_rows(
        got_feats.reshape(-1, features),
        got_grads.reshape(-1, features),
        gate_whole,
        up_whole,
        down_whole,
    )
    result = lax.psum(result, "dp").astype(jnp.bfloat16).reshape(senders, depth, features)
    arrived = lax.all_to_all(result, "expert", split_axis=0, concat_axis=0, tiled=True)
    slot_grad = arrived.reshape(experts * capacity, features)
    picked = slot_grad[slot_of_item].reshape(tokens, top_count, features).astype(jnp.float32)
    raised = jnp.exp(logits)
    weights = raised / jnp.sum(raised, axis=1, keepdims=True)
    combined = jnp.sum(weights[:, :, None] * picked, axis=1).astype(jnp.bfloat16)
    passed = shifted(combined, "section", -1)
    return passed[None]


MESH = pl.DeviceIdType.MESH


def dot(a, b, ca=1, cb=0):
    return lax.dot_general(a, b, (((ca,), (cb,)), ((), ())), preferred_element_type=jnp.float32)


def chain_kernel(
    n, sections, experts, cap, pieces,
    ids_ref, logits_ref, feat_hbm, grad_hbm, gate_hbm, up_hbm, down_hbm, out_ref,
    feat, grad, meta, rows_f, rows_g, send_f, send_g, res, res_in,
    part, part_send, up_in, dn_in, gate, up, down,
    own_sem, w_sem, w_send, w_recv,
    ag_recv, ag_up, ag_dn, y_send, y_recv, r_send, r_recv,
    p_send, up_recv, dn_recv, o_send, o_recv,
):
    top_count, tokens = ids_ref.shape
    features = feat_hbm.shape[0]
    me = lax.axis_index("expert")
    section = lax.axis_index("section")
    core = lax.rem(me, 2)
    e = me // 2
    y = lax.rem(e, 2)
    z = me // 4
    e_nb = e + 1 - 2 * y
    core_nb = {"expert": me + 1 - 2 * core}
    y_nb = {"expert": me + 2 - 4 * y}
    above, below = {"expert": me + 4}, {"expert": me - 4}
    before = {"section": lax.rem(section + sections - 1, sections)}
    after = {"section": lax.rem(section + 1, sections)}
    has_up, has_dn = z < n - 1, z > 0
    size = features // pieces

    barrier = pltpu.get_barrier_semaphore()
    for peer in (core_nb, y_nb, before, after):
        pl.semaphore_signal(barrier, inc=1, device_id=peer, device_id_type=MESH)

    @pl.when(has_up)
    def _():
        pl.semaphore_signal(barrier, inc=1, device_id=above, device_id_type=MESH)

    @pl.when(has_dn)
    def _():
        pl.semaphore_signal(barrier, inc=1, device_id=below, device_id_type=MESH)

    raised = jnp.exp(logits_ref[...])
    weights = raised / jnp.sum(raised, axis=0, keepdims=True)
    ids = ids_ref[...]
    expert_row = lax.broadcasted_iota(jnp.int32, (experts, tokens), 0)
    chosen = jnp.zeros((experts, tokens), jnp.float32)
    weight = jnp.zeros((experts, tokens), jnp.float32)
    for k in range(top_count):
        hit = jnp.where(ids[k : k + 1, :] == expert_row, 1.0, 0.0)
        chosen = chosen + hit
        weight = weight + hit * weights[k : k + 1, :]
    earlier = lax.broadcasted_iota(jnp.int32, (tokens, tokens), 0) < lax.broadcasted_iota(
        jnp.int32, (tokens, tokens), 1
    )
    place = dot(chosen.astype(jnp.bfloat16), jnp.where(earlier, 1.0, 0.0).astype(jnp.bfloat16))
    place = jnp.where(chosen > 0.5, place, -1.0)
    meta[z, :experts, :] = weight
    meta[z, experts:, :] = place

    own_copies = [
        pltpu.make_async_copy(feat_hbm, feat.at[z], own_sem.at[0]),
        pltpu.make_async_copy(grad_hbm, grad.at[z], own_sem.at[1]),
    ]
    for copy in own_copies:
        copy.start()
    w_copies = [
        pltpu.make_async_copy(src.at[0, 0], dst.at[0], w_sem.at[j])
        for j, (src, dst) in enumerate(((gate_hbm, gate), (up_hbm, up), (down_hbm, down)))
    ]
    for copy in w_copies:
        copy.start()

    pl.semaphore_wait(
        barrier, 4 + jnp.where(has_up, 1, 0) + jnp.where(has_dn, 1, 0)
    )

    def remote(src, dst, s_sem, r_sem, peer):
        return pltpu.make_async_remote_copy(
            src_ref=src, dst_ref=dst, send_sem=s_sem, recv_sem=r_sem,
            device_id=peer, device_id_type=MESH,
        )

    buffers = (feat, grad, meta)

    def hop(kind, b, upward, src=None):
        buf = buffers[kind].at[b]
        sems = ag_up if upward else ag_dn
        return remote(
            buf if src is None else src, buf, sems.at[kind, b], ag_recv.at[kind, b],
            above if upward else below,
        )

    sources = (feat_hbm, grad_hbm, None)
    for kind in (2, 0, 1):
        @pl.when(has_up)
        def _():
            hop(kind, z, True, sources[kind]).start()

        @pl.when(has_dn)
        def _():
            hop(kind, z, False, sources[kind]).start()

    swaps = [
        remote(src.at[0, 0], dst.at[1], w_send.at[j], w_recv.at[j], core_nb)
        for j, (src, dst) in enumerate(((gate_hbm, gate), (up_hbm, up), (down_hbm, down)))
    ]
    for copy in swaps:
        copy.start()

    def block_of(k):
        near = jnp.minimum(z, n - 1 - z)
        half = (k + 1) // 2
        side = jnp.where(lax.rem(k, 2) == 1, z - half, z + half)
        far = jnp.where(z < n - 1 - z, z + k - near, z - k + near)
        return jnp.where(k <= 2 * near, side, far)

    def passes(b):
        return jnp.logical_or(
            jnp.logical_and(b < z, has_up), jnp.logical_and(b > z, has_dn)
        )

    def forward(kind, k):
        b = block_of(k)

        @pl.when(passes(b))
        def _():
            if kind == 0:
                hop(2, b, True).wait_recv()
            hop(kind, b, True).wait_recv()

        for upward, there in ((True, jnp.logical_and(b < z, has_up)),
                              (False, jnp.logical_and(b > z, has_dn))):
            @pl.when(there)
            def _():
                if kind == 0:
                    hop(2, b, upward).start()
                hop(kind, b, upward).start()

    def forwards(kind, k):
        @pl.when(k == 1)
        def _():
            forward(kind, 1)

        @pl.when(jnp.logical_and(k >= 1, k < n - 1))
        def _():
            forward(kind, k + 1)

    def arrive(kind, b):
        @pl.when(jnp.logical_and(b != z, jnp.logical_not(passes(b))))
        def _():
            if kind == 0:
                hop(2, b, True).wait_recv()
            hop(kind, b, True).wait_recv()

        @pl.when(b == z)
        def _():
            own_copies[kind].wait()

    def y_copy(kind, b):
        src, dst = ((send_f, rows_f), (send_g, rows_g))[kind]
        return remote(
            src.at[b], dst.at[b, pl.ds(cap, cap)], y_send.at[kind, b], y_recv.at[kind, b], y_nb
        )

    def picks(b, expert):
        row = meta[b, pl.ds(experts + expert, 1), :]
        slot = lax.broadcasted_iota(jnp.int32, (cap, tokens), 0).astype(jnp.float32)
        return jnp.where(slot == row, 1.0, 0.0).astype(jnp.bfloat16)

    def stage_a(kind, k):
        b = block_of(k)
        whole, rows, sent = ((feat, rows_f, send_f), (grad, rows_g, send_g))[kind]
        arrive(kind, b)
        values = whole[b]
        sent[b] = dot(picks(b, e_nb), values, 1, 1).astype(jnp.bfloat16)
        y_copy(kind, b).start()
        rows[b, :cap, :] = dot(picks(b, e), values, 1, 1).astype(jnp.bfloat16)

    def r_copy(b):
        return remote(
            res.at[b, pl.ds(cap, cap)], res_in.at[b], r_send.at[b], r_recv.at[b], y_nb
        )

    def stage_b(k):
        b = block_of(k)

        @pl.when(k == 0)
        def _():
            for copy in w_copies:
                copy.wait()
            for copy in swaps:
                copy.wait_recv()

        y_copy(0, b).wait_recv()
        y_copy(1, b).wait_recv()

        def one_half(h, total):
            f, g = rows_f[b], rows_g[b]
            gate_pre = dot(f, gate[h])
            up_pre = dot(f, up[h])
            hidden_grad = dot(g, down[h], 1, 1)
            squash = jax.nn.sigmoid(swish_alpha * gate_pre)
            slope = squash + swish_alpha * gate_pre * squash * (1.0 - squash)
            gate_grad = (hidden_grad * (up_pre + 1.0) * slope).astype(jnp.bfloat16)
            up_grad = (hidden_grad * gate_pre * squash).astype(jnp.bfloat16)
            value = dot(gate_grad, gate[h], 1, 1) + dot(up_grad, up[h], 1, 1)
            return value if total is None else total + value

        total = one_half(1, one_half(0, None))
        res[b] = total.astype(jnp.bfloat16)
        r_copy(b).start()

    def p_copy(b, r, upward):
        rows = pl.ds(pl.multiple_of(r * size, size), size)
        dst, sems = (up_in, up_recv) if upward else (dn_in, dn_recv)
        return remote(
            part_send.at[b, rows], dst.at[b, rows], p_send.at[b, r], sems.at[b, r],
            above if upward else below,
        )

    def stage_c(k):
        b = block_of(k)
        r_copy(b).wait_recv()
        value = meta[b, pl.ds(e, 1), :] * dot(res[b, :cap, :], picks(b, e), 0, 0)
        value = value + meta[b, pl.ds(e_nb, 1), :] * dot(res_in[b], picks(b, e_nb), 0, 0)
        part[b] = value
        up_end = jnp.logical_and(b > z, jnp.logical_not(has_dn))
        dn_end = jnp.logical_and(b < z, jnp.logical_not(has_up))

        @pl.when(jnp.logical_or(up_end, dn_end))
        def _():
            part_send[b] = value.astype(jnp.bfloat16)

        @pl.when(up_end)
        def _():
            @pl.loop(0, pieces)
            def _(r):
                p_copy(b, r, True).start()

        @pl.when(dn_end)
        def _():
            @pl.loop(0, pieces)
            def _(r):
                p_copy(b, r, False).start()

    @pl.loop(0, n + 2)
    def _(k):
        forwards(0, k)

        @pl.when(k < n)
        def _():
            stage_a(0, k)

        @pl.when(k >= 2)
        def _():
            stage_c(k - 2)

        @pl.when(jnp.logical_and(k >= 1, k <= n))
        def _():
            stage_b(k - 1)

        forwards(1, k)

        @pl.when(k < n)
        def _():
            stage_a(1, k)

    def pass_on(b, upward):
        incoming = up_in if upward else dn_in

        @pl.loop(0, pieces)
        def _(r):
            rows = pl.ds(pl.multiple_of(r * size, size), size)
            p_copy(b, r, upward).wait_recv()
            value = part[b, rows, :] + incoming[b, rows, :].astype(jnp.float32)
            part_send[b, rows, :] = value.astype(jnp.bfloat16)
            p_copy(b, r, upward).start()

    def pass_up():
        @pl.loop(0, n)
        def _(b):
            @pl.when(jnp.logical_and(b > z, has_dn))
            def _():
                pass_on(b, True)

    @pl.when(z < n // 2)
    def _():
        pass_up()

    @pl.loop(0, n)
    def _(j):
        b = n - 1 - j

        @pl.when(jnp.logical_and(b < z, has_up))
        def _():
            pass_on(b, False)

    @pl.when(z >= n // 2)
    def _():
        pass_up()

    def o_copy(r):
        rows = pl.ds(pl.multiple_of(r * size, size), size)
        return remote(
            part_send.at[z, rows], out_ref.at[rows], o_send.at[r], o_recv.at[r], before
        )

    @pl.loop(0, pieces)
    def _(r):
        rows = pl.ds(pl.multiple_of(r * size, size), size)

        @pl.when(has_dn)
        def _():
            p_copy(z, r, True).wait_recv()
            part[z, rows, :] += up_in[z, rows, :].astype(jnp.float32)

        @pl.when(has_up)
        def _():
            p_copy(z, r, False).wait_recv()
            part[z, rows, :] += dn_in[z, rows, :].astype(jnp.float32)

        part_send[z, rows, :] = part[z, rows, :].astype(jnp.bfloat16)
        o_copy(r).start()

    for copy in swaps:
        copy.wait_send()

    @pl.loop(0, n)
    def _(b):
        @pl.when(jnp.logical_and(b <= z, has_up))
        def _():
            for kind in range(3):
                hop(kind, b, True).wait_send()

        @pl.when(jnp.logical_and(b >= z, has_dn))
        def _():
            for kind in range(3):
                hop(kind, b, False).wait_send()

        y_copy(0, b).wait_send()
        y_copy(1, b).wait_send()
        r_copy(b).wait_send()

        @pl.when(b != z)
        def _():
            @pl.loop(0, pieces)
            def _(r):
                p_copy(b, r, True).wait_send()

    @pl.loop(0, pieces)
    def _(r):
        o_copy(r).wait_send()
        o_copy(r).wait_recv()


def chained(saved_input, grad_output, expert_ids, router_logits, w_gate, w_up, w_down):
    _, tokens, features = saved_input.shape
    half = w_gate.shape[3]
    top_count = expert_ids.shape[2]
    slices = lax.axis_size("expert")
    experts = slices // 2
    n = slices // 4
    sections = lax.axis_size("section")
    capacity = min(tokens, tokens * top_count // experts * 17 // 16 // 2 * 2)
    cap = -(-capacity // 16) * 16
    pieces = max(p for p in range(1, 7) if features % (16 * p) == 0)
    bf16 = jnp.bfloat16
    dma = pltpu.SemaphoreType.DMA
    vmem, anywhere = pl.BlockSpec(memory_space=pltpu.VMEM), pl.BlockSpec(memory_space=pl.ANY)
    macs = 5 * 2 * n * cap * features * 2 * half
    passed = pl.pallas_call(
        functools.partial(chain_kernel, n, sections, experts, cap, pieces),
        out_shape=jax.ShapeDtypeStruct((features, tokens), bf16),
        in_specs=[vmem, vmem] + [anywhere] * 5,
        out_specs=anywhere,
        scratch_shapes=[
            pltpu.VMEM((n, features, tokens), bf16),
            pltpu.VMEM((n, features, tokens), bf16),
            pltpu.VMEM((n, 2 * experts, tokens), jnp.float32),
            pltpu.VMEM((n, 2 * cap, features), bf16),
            pltpu.VMEM((n, 2 * cap, features), bf16),
            pltpu.VMEM((n, cap, features), bf16),
            pltpu.VMEM((n, cap, features), bf16),
            pltpu.VMEM((n, 2 * cap, features), bf16),
            pltpu.VMEM((n, cap, features), bf16),
            pltpu.VMEM((n, features, tokens), jnp.float32),
            pltpu.VMEM((n, features, tokens), bf16),
            pltpu.VMEM((n, features, tokens), bf16),
            pltpu.VMEM((n, features, tokens), bf16),
            pltpu.VMEM((2, features, half), bf16),
            pltpu.VMEM((2, features, half), bf16),
            pltpu.VMEM((2, half, features), bf16),
            dma((2,)), dma((3,)), dma((3,)), dma((3,)),
            dma((3, n)), dma((3, n)), dma((3, n)),
            dma((2, n)), dma((2, n)), dma((n,)), dma((n,)),
            dma((n, pieces)), dma((n, pieces)), dma((n, pieces)),
            dma((pieces,)), dma((pieces,)),
        ],
        compiler_params=pltpu.CompilerParams(
            collective_id=0, has_side_effects=True, vmem_limit_bytes=58 * 1024 * 1024
        ),
        cost_estimate=pl.CostEstimate(
            flops=2 * macs, bytes_accessed=6 * half * features + 6 * tokens * features,
            transcendentals=4 * n * cap * half,
        ),
    )(
        expert_ids[0].T, router_logits[0].T, saved_input[0].T, grad_output[0].T,
        w_gate, w_up, w_down,
    )
    return passed.T[None]


def solution(mesh):
    placed = (
        P("section", ("groups", "expert"), None),
        P("section", ("groups", "expert"), None),
        P("section", ("groups", "expert"), None),
        P("section", ("groups", "expert"), None),
        P("section", "expert", None, "dp"),
        P("section", "expert", None, "dp"),
        P("section", "expert", "dp", None),
    )
    shape = dict(mesh.shape)
    chain = shape["dp"] == 1 and shape["expert"] % 4 == 0 and shape["section"] > 1
    return jax.shard_map(
        chained if chain else on_device,
        mesh=mesh,
        in_specs=placed,
        out_specs=P("section", ("groups", "expert"), None),
        check_vma=False,
    )
```

```python
import functools

import jax
import jax.numpy as jnp
from jax import lax
from jax.experimental import pallas as pl
from jax.experimental.pallas import tpu as pltpu
from jax.sharding import PartitionSpec as P

swish_alpha = 1.702


def swapped(value, axis, stride):
    mask = 2**stride
    pairs = [(source, source ^ mask) for source in range(lax.axis_size(axis))]
    return lax.ppermute(value, axis, pairs)


def shifted(block, axis, distance):
    devices = range(lax.axis_size(axis))
    route = [((i - distance) % len(devices), i) for i in devices]
    return lax.ppermute(block, axis, route)


def expert_rows(feat_rows, grad_rows, gate_mat, up_mat, down_mat):
    gate_pre = jnp.dot(feat_rows, gate_mat, preferred_element_type=jnp.float32)
    up_pre = jnp.dot(feat_rows, up_mat, preferred_element_type=jnp.float32)
    hidden_grad = lax.dot_general(
        grad_rows, down_mat, (((1,), (1,)), ((), ())), preferred_element_type=jnp.float32
    )
    squash = jax.nn.sigmoid(swish_alpha * gate_pre)
    slope = squash + swish_alpha * gate_pre * squash * (1.0 - squash)
    gate_grad = (hidden_grad * (up_pre + 1.0) * slope).astype(jnp.bfloat16)
    up_grad = (hidden_grad * gate_pre * squash).astype(jnp.bfloat16)
    first = lax.dot_general(
        gate_grad, gate_mat, (((1,), (1,)), ((), ())), preferred_element_type=jnp.float32
    )
    second = lax.dot_general(
        up_grad, up_mat, (((1,), (1,)), ((), ())), preferred_element_type=jnp.float32
    )
    return first + second


def on_device(saved_input, grad_output, expert_ids, router_logits, w_gate, w_up, w_down):
    gate_half = w_gate[0, 0]
    up_half = w_up[0, 0]
    down_half = w_down[0, 0]
    feat_rows = saved_input[0]
    grad_rows = grad_output[0]
    chosen = expert_ids[0]
    logits = router_logits[0]
    tokens, features = feat_rows.shape
    top_count = chosen.shape[1]
    slices = lax.axis_size("expert")
    experts = slices // 2
    capacity = min(tokens, tokens * top_count // experts * 17 // 16 // 2 * 2)
    half_cap = capacity // 2
    entries = chosen.reshape(-1)
    total_items = entries.shape[0]
    onehot = (entries[:, None] == jnp.arange(experts, dtype=jnp.int32)[None, :]).astype(jnp.int32)
    before = jnp.cumsum(onehot, axis=0) - onehot
    position = jnp.sum(before * onehot, axis=1)
    slot_of_item = entries * capacity + position
    item_of_slot = jnp.full((experts * capacity,), total_items, jnp.int32)
    item_of_slot = item_of_slot.at[slot_of_item].set(jnp.arange(total_items, dtype=jnp.int32))
    occupied = (item_of_slot < total_items)[:, None]
    source = jnp.where(item_of_slot < total_items, item_of_slot // top_count, 0)
    zero_value = jnp.zeros((), jnp.bfloat16)
    send_feats = jnp.where(occupied, feat_rows[source], zero_value).reshape(
        experts, capacity, features
    )
    send_grads = jnp.where(occupied, grad_rows[source], zero_value).reshape(
        experts, capacity, features
    )
    other_gate, other_up, other_down = swapped((gate_half, up_half, down_half), "expert", 0)
    gate_whole = jnp.concatenate([gate_half, other_gate], axis=1)
    up_whole = jnp.concatenate([up_half, other_up], axis=1)
    down_whole = jnp.concatenate([down_half, other_down], axis=0)
    split_feats = send_feats.reshape(slices, half_cap, features)
    split_grads = send_grads.reshape(slices, half_cap, features)
    got_feats = lax.all_to_all(split_feats, "expert", split_axis=0, concat_axis=0, tiled=True)
    got_grads = lax.all_to_all(split_grads, "expert", split_axis=0, concat_axis=0, tiled=True)
    senders, depth, _ = got_feats.shape
    result = expert_rows(
        got_feats.reshape(-1, features),
        got_grads.reshape(-1, features),
        gate_whole,
        up_whole,
        down_whole,
    )
    result = lax.psum(result, "dp").astype(jnp.bfloat16).reshape(senders, depth, features)
    arrived = lax.all_to_all(result, "expert", split_axis=0, concat_axis=0, tiled=True)
    slot_grad = arrived.reshape(experts * capacity, features)
    picked = slot_grad[slot_of_item].reshape(tokens, top_count, features).astype(jnp.float32)
    raised = jnp.exp(logits)
    weights = raised / jnp.sum(raised, axis=1, keepdims=True)
    combined = jnp.sum(weights[:, :, None] * picked, axis=1).astype(jnp.bfloat16)
    passed = shifted(combined, "section", -1)
    return passed[None]


MESH = pl.DeviceIdType.MESH


def dot(a, b, ca=1, cb=0):
    return lax.dot_general(a, b, (((ca,), (cb,)), ((), ())), preferred_element_type=jnp.float32)


def chain_kernel(
    n, sections, experts, cap, pieces,
    ids_ref, logits_ref, feat_hbm, grad_hbm, gate_hbm, up_hbm, down_hbm, out_ref,
    feat, grad, meta, rows_f, rows_g, send_f, send_g, res, res_in,
    part, part_send, up_in, dn_in, gate, up, down, for_gate, for_up,
    own_sem, w_sem, w_send, w_recv,
    ag_recv, ag_up, ag_dn, y_send, y_recv, r_send, r_recv,
    p_send, up_recv, dn_recv, o_send, o_recv,
):
    top_count, tokens = ids_ref.shape
    features = feat_hbm.shape[0]
    me = lax.axis_index("expert")
    section = lax.axis_index("section")
    core = lax.rem(me, 2)
    e = me // 2
    y = lax.rem(e, 2)
    z = me // 4
    e_nb = e + 1 - 2 * y
    core_nb = {"expert": me + 1 - 2 * core}
    y_nb = {"expert": me + 2 - 4 * y}
    above, below = {"expert": me + 4}, {"expert": me - 4}
    before = {"section": lax.rem(section + sections - 1, sections)}
    after = {"section": lax.rem(section + 1, sections)}
    has_up, has_dn = z < n - 1, z > 0
    size = features // pieces

    barrier = pltpu.get_barrier_semaphore()
    for peer in (core_nb, y_nb, before, after):
        pl.semaphore_signal(barrier, inc=1, device_id=peer, device_id_type=MESH)

    @pl.when(has_up)
    def _():
        pl.semaphore_signal(barrier, inc=1, device_id=above, device_id_type=MESH)

    @pl.when(has_dn)
    def _():
        pl.semaphore_signal(barrier, inc=1, device_id=below, device_id_type=MESH)

    raised = jnp.exp(logits_ref[...])
    weights = raised / jnp.sum(raised, axis=0, keepdims=True)
    ids = ids_ref[...]
    expert_row = lax.broadcasted_iota(jnp.int32, (experts, tokens), 0)
    chosen = jnp.zeros((experts, tokens), jnp.float32)
    weight = jnp.zeros((experts, tokens), jnp.float32)
    for k in range(top_count):
        hit = jnp.where(ids[k : k + 1, :] == expert_row, 1.0, 0.0)
        chosen = chosen + hit
        weight = weight + hit * weights[k : k + 1, :]
    earlier = lax.broadcasted_iota(jnp.int32, (tokens, tokens), 0) < lax.broadcasted_iota(
        jnp.int32, (tokens, tokens), 1
    )
    place = dot(chosen.astype(jnp.bfloat16), jnp.where(earlier, 1.0, 0.0).astype(jnp.bfloat16))
    place = jnp.where(chosen > 0.5, place, -1.0)
    meta[z, :experts, :] = weight
    meta[z, experts:, :] = place

    own_copies = [
        pltpu.make_async_copy(feat_hbm, feat.at[z], own_sem.at[0]),
        pltpu.make_async_copy(grad_hbm, grad.at[z], own_sem.at[1]),
    ]
    for copy in own_copies:
        copy.start()
    w_copies = [
        pltpu.make_async_copy(src.at[0, 0], dst.at[0], w_sem.at[j])
        for j, (src, dst) in enumerate(((gate_hbm, gate), (up_hbm, up), (down_hbm, down)))
    ]
    for copy in w_copies:
        copy.start()

    pl.semaphore_wait(
        barrier, 4 + jnp.where(has_up, 1, 0) + jnp.where(has_dn, 1, 0)
    )

    def remote(src, dst, s_sem, r_sem, peer):
        return pltpu.make_async_remote_copy(
            src_ref=src, dst_ref=dst, send_sem=s_sem, recv_sem=r_sem,
            device_id=peer, device_id_type=MESH,
        )

    buffers = (feat, grad, meta)

    def hop(kind, b, upward, src=None):
        buf = buffers[kind].at[b]
        sems = ag_up if upward else ag_dn
        return remote(
            buf if src is None else src, buf, sems.at[kind, b], ag_recv.at[kind, b],
            above if upward else below,
        )

    sources = (feat_hbm, grad_hbm, None)
    for kind in (2, 0, 1):
        @pl.when(has_up)
        def _():
            hop(kind, z, True, sources[kind]).start()

        @pl.when(has_dn)
        def _():
            hop(kind, z, False, sources[kind]).start()

    swaps = [
        remote(src.at[0, 0], dst.at[1], w_send.at[j], w_recv.at[j], core_nb)
        for j, (src, dst) in enumerate(((gate_hbm, gate), (up_hbm, up), (down_hbm, down)))
    ]
    for copy in swaps:
        copy.start()

    def block_of(k):
        near = jnp.minimum(z, n - 1 - z)
        half = (k + 1) // 2
        side = jnp.where(lax.rem(k, 2) == 1, z - half, z + half)
        far = jnp.where(z < n - 1 - z, z + k - near, z - k + near)
        return jnp.where(k <= 2 * near, side, far)

    def passes(b):
        return jnp.logical_or(
            jnp.logical_and(b < z, has_up), jnp.logical_and(b > z, has_dn)
        )

    def forward(kind, k):
        b = block_of(k)

        @pl.when(passes(b))
        def _():
            if kind == 0:
                hop(2, b, True).wait_recv()
            hop(kind, b, True).wait_recv()

        for upward, there in ((True, jnp.logical_and(b < z, has_up)),
                              (False, jnp.logical_and(b > z, has_dn))):
            @pl.when(there)
            def _():
                if kind == 0:
                    hop(2, b, upward).start()
                hop(kind, b, upward).start()

    def forwards(kind, k):
        @pl.when(k == 1)
        def _():
            forward(kind, 1)

        @pl.when(jnp.logical_and(k >= 1, k < n - 1))
        def _():
            forward(kind, k + 1)

    def arrive(kind, b):
        @pl.when(jnp.logical_and(b != z, jnp.logical_not(passes(b))))
        def _():
            if kind == 0:
                hop(2, b, True).wait_recv()
            hop(kind, b, True).wait_recv()

        @pl.when(b == z)
        def _():
            own_copies[kind].wait()

    def y_copy(kind, b):
        src, dst = ((send_f, rows_f), (send_g, rows_g))[kind]
        return remote(
            src.at[b], dst.at[b, pl.ds(cap, cap)], y_send.at[kind, b], y_recv.at[kind, b], y_nb
        )

    def picks(b, expert):
        row = meta[b, pl.ds(experts + expert, 1), :]
        slot = lax.broadcasted_iota(jnp.int32, (cap, tokens), 0).astype(jnp.float32)
        return jnp.where(slot == row, 1.0, 0.0).astype(jnp.bfloat16)

    def stage_a(kind, k):
        b = block_of(k)
        whole, rows, sent = ((feat, rows_f, send_f), (grad, rows_g, send_g))[kind]
        arrive(kind, b)
        values = whole[b]
        sent[b] = dot(picks(b, e_nb), values, 1, 1).astype(jnp.bfloat16)
        y_copy(kind, b).start()
        rows[b, :cap, :] = dot(picks(b, e), values, 1, 1).astype(jnp.bfloat16)

    def r_copy(b):
        return remote(
            res.at[b, pl.ds(cap, cap)], res_in.at[b], r_send.at[b], r_recv.at[b], y_nb
        )

    def weights_in(k, which):
        @pl.when(k == 0)
        def _():
            for j in which:
                w_copies[j].wait()
            for j in which:
                swaps[j].wait_recv()

    def stage_bf(k):
        b = block_of(k)
        weights_in(k, (0, 1))
        y_copy(0, b).wait_recv()
        for h in range(2):
            f = rows_f[b]
            gate_pre = dot(f, gate[h])
            up_pre = dot(f, up[h])
            squash = jax.nn.sigmoid(swish_alpha * gate_pre)
            slope = squash + swish_alpha * gate_pre * squash * (1.0 - squash)
            for_gate[h] = (up_pre + 1.0) * slope
            for_up[h] = gate_pre * squash

    def stage_bg(k):
        b = block_of(k)
        weights_in(k, (2,))
        y_copy(1, b).wait_recv()
        total = None
        for h in range(2):
            hidden_grad = dot(rows_g[b], down[h], 1, 1)
            gate_grad = (hidden_grad * for_gate[h]).astype(jnp.bfloat16)
            up_grad = (hidden_grad * for_up[h]).astype(jnp.bfloat16)
            value = dot(gate_grad, gate[h], 1, 1) + dot(up_grad, up[h], 1, 1)
            total = value if total is None else total + value
        res[b] = total.astype(jnp.bfloat16)
        r_copy(b).start()

    def p_copy(b, r, upward):
        rows = pl.ds(pl.multiple_of(r * size, size), size)
        dst, sems = (up_in, up_recv) if upward else (dn_in, dn_recv)
        return remote(
            part_send.at[b, rows], dst.at[b, rows], p_send.at[b, r], sems.at[b, r],
            above if upward else below,
        )

    def stage_c(k):
        b = block_of(k)
        r_copy(b).wait_recv()
        value = meta[b, pl.ds(e, 1), :] * dot(res[b, :cap, :], picks(b, e), 0, 0)
        value = value + meta[b, pl.ds(e_nb, 1), :] * dot(res_in[b], picks(b, e_nb), 0, 0)
        part[b] = value
        up_end = jnp.logical_and(b > z, jnp.logical_not(has_dn))
        dn_end = jnp.logical_and(b < z, jnp.logical_not(has_up))

        @pl.when(jnp.logical_or(up_end, dn_end))
        def _():
            part_send[b] = value.astype(jnp.bfloat16)

        @pl.when(up_end)
        def _():
            @pl.loop(0, pieces)
            def _(r):
                p_copy(b, r, True).start()

        @pl.when(dn_end)
        def _():
            @pl.loop(0, pieces)
            def _(r):
                p_copy(b, r, False).start()

    @pl.loop(0, n + 1)
    def _(k):
        forwards(0, k)

        @pl.when(k < n)
        def _():
            stage_a(0, k)

        @pl.when(k >= 1)
        def _():
            stage_bg(k - 1)

        forwards(1, k)

        @pl.when(k < n)
        def _():
            stage_a(1, k)
            stage_bf(k)

        @pl.when(k >= 1)
        def _():
            stage_c(k - 1)

    def pass_on(b, upward):
        incoming = up_in if upward else dn_in

        @pl.loop(0, pieces)
        def _(r):
            rows = pl.ds(pl.multiple_of(r * size, size), size)
            p_copy(b, r, upward).wait_recv()
            value = part[b, rows, :] + incoming[b, rows, :].astype(jnp.float32)
            part_send[b, rows, :] = value.astype(jnp.bfloat16)
            p_copy(b, r, upward).start()

    def pass_up():
        @pl.loop(0, n)
        def _(b):
            @pl.when(jnp.logical_and(b > z, has_dn))
            def _():
                pass_on(b, True)

    @pl.when(z < n // 2)
    def _():
        pass_up()

    @pl.loop(0, n)
    def _(j):
        b = n - 1 - j

        @pl.when(jnp.logical_and(b < z, has_up))
        def _():
            pass_on(b, False)

    @pl.when(z >= n // 2)
    def _():
        pass_up()

    def o_copy(r):
        rows = pl.ds(pl.multiple_of(r * size, size), size)
        return remote(
            part_send.at[z, rows], out_ref.at[rows], o_send.at[r], o_recv.at[r], before
        )

    @pl.loop(0, pieces)
    def _(r):
        rows = pl.ds(pl.multiple_of(r * size, size), size)

        @pl.when(has_dn)
        def _():
            p_copy(z, r, True).wait_recv()
            part[z, rows, :] += up_in[z, rows, :].astype(jnp.float32)

        @pl.when(has_up)
        def _():
            p_copy(z, r, False).wait_recv()
            part[z, rows, :] += dn_in[z, rows, :].astype(jnp.float32)

        part_send[z, rows, :] = part[z, rows, :].astype(jnp.bfloat16)
        o_copy(r).start()

    for copy in swaps:
        copy.wait_send()

    @pl.loop(0, n)
    def _(b):
        @pl.when(jnp.logical_and(b <= z, has_up))
        def _():
            for kind in range(3):
                hop(kind, b, True).wait_send()

        @pl.when(jnp.logical_and(b >= z, has_dn))
        def _():
            for kind in range(3):
                hop(kind, b, False).wait_send()

        y_copy(0, b).wait_send()
        y_copy(1, b).wait_send()
        r_copy(b).wait_send()

        @pl.when(b != z)
        def _():
            @pl.loop(0, pieces)
            def _(r):
                p_copy(b, r, True).wait_send()

    @pl.loop(0, pieces)
    def _(r):
        o_copy(r).wait_send()
        o_copy(r).wait_recv()


def chained(saved_input, grad_output, expert_ids, router_logits, w_gate, w_up, w_down):
    _, tokens, features = saved_input.shape
    half = w_gate.shape[3]
    top_count = expert_ids.shape[2]
    slices = lax.axis_size("expert")
    experts = slices // 2
    n = slices // 4
    sections = lax.axis_size("section")
    capacity = min(tokens, tokens * top_count // experts * 17 // 16 // 2 * 2)
    cap = -(-capacity // 16) * 16
    pieces = max(p for p in range(1, 7) if features % (16 * p) == 0)
    bf16 = jnp.bfloat16
    dma = pltpu.SemaphoreType.DMA
    vmem, anywhere = pl.BlockSpec(memory_space=pltpu.VMEM), pl.BlockSpec(memory_space=pl.ANY)
    macs = 5 * 2 * n * cap * features * 2 * half
    passed = pl.pallas_call(
        functools.partial(chain_kernel, n, sections, experts, cap, pieces),
        out_shape=jax.ShapeDtypeStruct((features, tokens), bf16),
        in_specs=[vmem, vmem] + [anywhere] * 5,
        out_specs=anywhere,
        scratch_shapes=[
            pltpu.VMEM((n, features, tokens), bf16),
            pltpu.VMEM((n, features, tokens), bf16),
            pltpu.VMEM((n, 2 * experts, tokens), jnp.float32),
            pltpu.VMEM((n, 2 * cap, features), bf16),
            pltpu.VMEM((n, 2 * cap, features), bf16),
            pltpu.VMEM((n, cap, features), bf16),
            pltpu.VMEM((n, cap, features), bf16),
            pltpu.VMEM((n, 2 * cap, features), bf16),
            pltpu.VMEM((n, cap, features), bf16),
            pltpu.VMEM((n, features, tokens), jnp.float32),
            pltpu.VMEM((n, features, tokens), bf16),
            pltpu.VMEM((n, features, tokens), bf16),
            pltpu.VMEM((n, features, tokens), bf16),
            pltpu.VMEM((2, features, half), bf16),
            pltpu.VMEM((2, features, half), bf16),
            pltpu.VMEM((2, half, features), bf16),
            pltpu.VMEM((2, 2 * cap, half), jnp.float32),
            pltpu.VMEM((2, 2 * cap, half), jnp.float32),
            dma((2,)), dma((3,)), dma((3,)), dma((3,)),
            dma((3, n)), dma((3, n)), dma((3, n)),
            dma((2, n)), dma((2, n)), dma((n,)), dma((n,)),
            dma((n, pieces)), dma((n, pieces)), dma((n, pieces)),
            dma((pieces,)), dma((pieces,)),
        ],
        compiler_params=pltpu.CompilerParams(
            collective_id=0, has_side_effects=True, vmem_limit_bytes=58 * 1024 * 1024
        ),
        cost_estimate=pl.CostEstimate(
            flops=2 * macs, bytes_accessed=6 * half * features + 6 * tokens * features,
            transcendentals=4 * n * cap * half,
        ),
    )(
        expert_ids[0].T, router_logits[0].T, saved_input[0].T, grad_output[0].T,
        w_gate, w_up, w_down,
    )
    return passed.T[None]


def solution(mesh):
    placed = (
        P("section", ("groups", "expert"), None),
        P("section", ("groups", "expert"), None),
        P("section", ("groups", "expert"), None),
        P("section", ("groups", "expert"), None),
        P("section", "expert", None, "dp"),
        P("section", "expert", None, "dp"),
        P("section", "expert", "dp", None),
    )
    shape = dict(mesh.shape)
    chain = shape["dp"] == 1 and shape["expert"] % 4 == 0 and shape["section"] > 1
    return jax.shard_map(
        chained if chain else on_device,
        mesh=mesh,
        in_specs=placed,
        out_specs=P("section", ("groups", "expert"), None),
        check_vma=False,
    )
```
